32 devices in a mesh: groups: 2 (over y), tensor: 4 (over z), dp: 4 (over x, core).
Axes of the slice: x: 2, y: 2, z: 4, core: 2. Of those that a mesh axis runs over, the one named last changes fastest.
Arguments:
- incoming_entries: bfloat16 [256, 4608], P(('groups', 'tensor'), 'dp'), parts along dimension 0, may hold values from -6 to 6
- output_adjoint: bfloat16 [256, 4608], P(('groups', 'tensor'), 'dp'), parts along dimension 0, may hold values from -1.5 to 1.5
- remaining_members: int32 [3], replicated, may hold values from 0 to 3, as said below
- gating_matrix: bfloat16 [4608, 18432], P('dp', 'tensor'), may hold values from -0.09375 to 0.09375
- expansion_matrix: bfloat16 [4608, 18432], P('dp', 'tensor'), may hold values from -0.09375 to 0.09375
- contraction_matrix: bfloat16 [18432, 4608], P('tensor', 'dp'), may hold values from -0.046875 to 0.046875
Outputs:
- grad_tokens: bfloat16 [256, 4608], P(('groups', 'tensor'), 'dp'), parts along dimension 0
- grad_gate: bfloat16 [9216, 18432], P(('groups', 'dp'), 'tensor'), parts along dimension 0
- grad_up: bfloat16 [9216, 18432], P(('groups', 'dp'), 'tensor'), parts along dimension 0
- grad_down: bfloat16 [36864, 4608], P(('groups', 'tensor'), 'dp'), parts along dimension 0
The draws below stay inside these ranges and needn't reach their ends.
There are 2 independent parts, one for each index of `groups`. The reference program is written for one: setup_inputs(seed, part) draws one part's arguments, and reference() takes and returns one part's arrays. A program takes and returns all parts, laid end to end along the dimension named above; an argument that names none is the same for every part. Nothing has to cross between parts.
Inputs may be any that keep to these rules, and one draw needn't show every extreme that they name: `remaining_members`: 3 distinct ranks of the tensor axis, rank 0 and rank 4 - 1 among them; the hidden units of the other ranks' blocks are switched off.
All inputs are finite; a program needn't handle non-finite values.
Results may differ from the reference program's by a relative error of at most 0.02.
Values may be sent and summed in bfloat16 or wider, within the bound.
A program may use at most 192 MiB of HBM per device.

```python
import math
import jax
import jax.numpy as jnp
from jax import lax

D = 4608
FF = 18432
TOKENS = 128
ALIVE = 3
N_TENSOR = 4
N_DP = 4


def draw_remaining_members(key, part):
    key = jax.random.fold_in(key, 7)
    inner_key = jax.random.fold_in(key, 1)
    order_key = jax.random.fold_in(key, 2)
    inner_ranks = jax.random.permutation(inner_key, N_TENSOR - 2).astype(jnp.int32) + 1
    chosen = jnp.concatenate([jnp.array([0, N_TENSOR - 1], dtype=jnp.int32), inner_ranks[:ALIVE - 2]])
    return jax.random.permutation(order_key, chosen).astype(jnp.int32)


def levels(own_key, extent, pieces, smallest, top_value):
    level, own = 1.0, jax.random.fold_in(own_key, 6)
    for position, blocks in pieces:
        heights = jnp.exp(jax.random.uniform(jax.random.fold_in(own, position), (blocks,), jnp.float32, smallest / len(pieces), top_value / len(pieces)))
        level = level * jnp.repeat(heights, extent[position] // blocks).reshape([-1 if axis == position else 1 for axis in range(len(extent))])
    return level


def bell_draw(rng, extent, width, bound, split=(), kind=jnp.bfloat16):
    entries = width * jax.random.normal(rng, extent, jnp.float32)
    if split:
        entries = entries * levels(rng, extent, split, -0.22, 0.18)
    return jnp.clip(entries, -bound, bound).astype(kind)


def setup_inputs(seed: int = 0, part: int = 0) -> dict:
    seeds = jax.random.split(jax.random.key(seed), 7)
    part_keys = jax.random.split(jax.random.fold_in(seeds[6], part), 7)
    return {
        "incoming_entries": bell_draw(part_keys[0], (TOKENS, D), 1.0, 6.0, ((0, 4), (1, 4))),
        "output_adjoint": bell_draw(part_keys[1], (TOKENS, D), 0.25, 1.5, ((0, 4), (1, 4))),
        "remaining_members": draw_remaining_members(jax.random.fold_in(seeds[6], 71), part),
        "gating_matrix": bell_draw(seeds[3], (D, FF), D ** -0.5, 0.09375, ((0, 4), (1, 4))),
        "expansion_matrix": bell_draw(seeds[4], (D, FF), D ** -0.5, 0.09375, ((0, 4), (1, 4))),
        "contraction_matrix": bell_draw(seeds[5], (FF, D), FF ** -0.5, 0.046875, ((0, 4), (1, 4))),
    }


cubic_coef = 0.044715

def gelu_pair(pre_act):
    tanh_scale = math.sqrt(2.0 / math.pi)
    tangent = jnp.tanh(tanh_scale * (pre_act + cubic_coef * pre_act * pre_act * pre_act))
    active = 0.5 * pre_act * (1.0 + tangent)
    slope_val = 0.5 * (1.0 + tangent) + 0.5 * pre_act * (1.0 - tangent * tangent) * tanh_scale * (1.0 + 3.0 * cubic_coef * pre_act * pre_act)
    return (active, slope_val)

def rounded(term):
    return lax.optimization_barrier(term.astype(jnp.bfloat16)).astype(jnp.float32)

def reference(incoming_entries, output_adjoint, remaining_members, gating_matrix, expansion_matrix, contraction_matrix):
    width_dev = D // N_DP
    gate_sum = jnp.zeros((TOKENS, FF), jnp.float32)
    up_sum = jnp.zeros((TOKENS, FF), jnp.float32)
    back_sum = jnp.zeros((TOKENS, FF), jnp.float32)
    for piece_index in range(N_DP):
        offset = piece_index * width_dev
        tok_cols = incoming_entries[:, offset:offset + width_dev]
        cot_cols = output_adjoint[:, offset:offset + width_dev]
        gate_sum = gate_sum + rounded(jnp.dot(tok_cols, gating_matrix[offset:offset + width_dev], preferred_element_type=jnp.float32))
        up_sum = up_sum + rounded(jnp.dot(tok_cols, expansion_matrix[offset:offset + width_dev], preferred_element_type=jnp.float32))
        back_sum = back_sum + rounded(jnp.dot(cot_cols, contraction_matrix[:, offset:offset + width_dev].T, preferred_element_type=jnp.float32))
    latent_group_index = jnp.arange(FF, dtype=jnp.int32) // (FF // N_TENSOR)
    retained_markers = jnp.any(latent_group_index[:, None] == remaining_members[None, :].astype(jnp.int32), axis=1).astype(jnp.float32)
    active, slope_val = gelu_pair(gate_sum)
    hidden = (retained_markers * active * up_sum).astype(jnp.bfloat16)
    gate_grad = (retained_markers * back_sum * up_sum * slope_val).astype(jnp.bfloat16)
    up_grad = (retained_markers * back_sum * active).astype(jnp.bfloat16)
    grad_gate = jnp.dot(incoming_entries.T, gate_grad, preferred_element_type=jnp.float32).astype(jnp.bfloat16)
    grad_up = jnp.dot(incoming_entries.T, up_grad, preferred_element_type=jnp.float32).astype(jnp.bfloat16)
    grad_down = jnp.dot(hidden.T, output_adjoint, preferred_element_type=jnp.float32).astype(jnp.bfloat16)
    input_sum = jnp.dot(gate_grad, gating_matrix.T, preferred_element_type=jnp.float32) + jnp.dot(up_grad, expansion_matrix.T, preferred_element_type=jnp.float32)
    return (input_sum.astype(jnp.bfloat16), grad_gate, grad_up, grad_down)
```

```python
import functools
import math

import jax
import jax.numpy as jnp
from jax import lax
from jax.experimental import pallas as pl
from jax.experimental.pallas import tpu as pltpu
from jax.sharding import PartitionSpec as P

cubic_coef = 0.044715


def gelu_pair(pre_act):
    tanh_scale = math.sqrt(2.0 / math.pi)
    tangent = jnp.tanh(tanh_scale * (pre_act + cubic_coef * pre_act * pre_act * pre_act))
    active = 0.5 * pre_act * (1.0 + tangent)
    slope_val = 0.5 * (1.0 + tangent) + 0.5 * pre_act * (1.0 - tangent * tangent) * tanh_scale * (
        1.0 + 3.0 * cubic_coef * pre_act * pre_act
    )
    return (active, slope_val)


def activate(totals, retained_marker):
    gate_sum = totals[:, 0]
    up_sum = totals[:, 1]
    back_sum = totals[:, 2]
    active, slope_val = gelu_pair(gate_sum)
    hidden = (retained_marker * active * up_sum).astype(jnp.bfloat16)
    gate_grad = (retained_marker * back_sum * up_sum * slope_val).astype(jnp.bfloat16)
    up_grad = (retained_marker * back_sum * active).astype(jnp.bfloat16)
    return (hidden, gate_grad, up_grad)


def plain_body(
    incoming_entries,
    output_adjoint,
    remaining_members,
    gating_matrix,
    expansion_matrix,
    contraction_matrix,
):
    cycle_location = lax.axis_index("tensor")
    retained_marker = jnp.sum((remaining_members == cycle_location).astype(jnp.float32))
    tok_all, cot_all = (
        lax.all_gather(incoming_entries, "tensor", axis=0, tiled=True),
        lax.all_gather(output_adjoint, "tensor", axis=0, tiled=True),
    )
    gate_part = jnp.dot(tok_all, gating_matrix, preferred_element_type=jnp.float32)
    up_part = jnp.dot(tok_all, expansion_matrix, preferred_element_type=jnp.float32)
    back_part = lax.dot_general(
        cot_all, contraction_matrix, (((1,), (1,)), ((), ())), preferred_element_type=jnp.float32
    )
    totals = lax.psum_scatter(
        jnp.stack([gate_part, up_part, back_part], axis=1).astype(jnp.bfloat16),
        "dp",
        scatter_dimension=0,
        tiled=True,
    ).astype(jnp.float32)
    hidden_loc, gate_loc, up_loc = activate(totals, retained_marker)
    hidden, gate_grad, up_grad = (
        lax.all_gather(hidden_loc, "dp", axis=0, tiled=True),
        lax.all_gather(gate_loc, "dp", axis=0, tiled=True),
        lax.all_gather(up_loc, "dp", axis=0, tiled=True),
    )
    over_rows = (((0,), (0,)), ((), ()))
    grad_gate = lax.dot_general(
        tok_all, gate_grad, over_rows, preferred_element_type=jnp.float32
    ).astype(jnp.bfloat16)
    grad_up = lax.dot_general(
        tok_all, up_grad, over_rows, preferred_element_type=jnp.float32
    ).astype(jnp.bfloat16)
    grad_down = lax.dot_general(
        hidden, cot_all, over_rows, preferred_element_type=jnp.float32
    ).astype(jnp.bfloat16)
    over_units = (((1,), (1,)), ((), ()))
    first = lax.dot_general(
        gate_grad, gating_matrix, over_units, preferred_element_type=jnp.float32
    )
    second = lax.dot_general(
        up_grad, expansion_matrix, over_units, preferred_element_type=jnp.float32
    )
    grad_tokens = lax.psum_scatter(
        (first + second).astype(jnp.bfloat16), "tensor", scatter_dimension=0, tiled=True
    )
    return (grad_tokens, grad_gate, grad_up, grad_down)


MESH = pl.DeviceIdType.MESH
NT = (((1,), (1,)), ((), ()))
TN = (((0,), (0,)), ((), ()))


def exchange_kernel(
    n_z,
    n_chunks,
    tok_ref,
    cot_ref,
    members_ref,
    wg_hbm,
    wu_hbm,
    wd_hbm,
    tok_all,
    cot_all,
    h_all,
    *rest,
):
    blocks = rest[:n_z]
    (
        wg, wu, wd, mine, csend, crecv, xsend, xrecv, acc,
        w_sem, z_send, z_recv, c_send, c_recv, x_send, x_recv, h_send, h_recv,
    ) = rest[n_z:]
    rows = tok_ref.shape[0]
    half = mine.shape[2]
    width = wg.shape[2]
    me_z = lax.axis_index("tensor")
    me_d = lax.axis_index("dp")
    core = lax.rem(me_d, 2)
    other_core = me_d + 1 - 2 * core
    other_chip = lax.rem(me_d + 2, 4)

    def weight_copies(c):
        cols = pl.ds(pl.multiple_of(c * width, width), width)
        return (
            pltpu.make_async_copy(wg_hbm.at[:, cols], wg.at[c], w_sem.at[0, c]),
            pltpu.make_async_copy(wu_hbm.at[:, cols], wu.at[c], w_sem.at[1, c]),
            pltpu.make_async_copy(wd_hbm.at[cols, :], wd.at[c], w_sem.at[2, c]),
        )

    @pl.loop(0, n_chunks)
    def _(c):
        for copy in weight_copies(c):
            copy.start()

    barrier = pltpu.get_barrier_semaphore()
    for k in range(1, n_z):
        pl.semaphore_signal(
            barrier, inc=1, device_id={"tensor": lax.rem(me_z + k, n_z)}, device_id_type=MESH
        )
    pl.semaphore_signal(barrier, inc=1, device_id={"dp": other_core}, device_id_type=MESH)
    pl.semaphore_signal(barrier, inc=1, device_id={"dp": other_chip}, device_id_type=MESH)
    pl.semaphore_wait(barrier, n_z + 1)

    own_rows = pl.ds(pl.multiple_of(me_z * rows, rows), rows)

    def gather_copy(which, k):
        src, dst = ((tok_ref, tok_all), (cot_ref, cot_all))[which]
        return pltpu.make_async_remote_copy(
            src_ref=src,
            dst_ref=dst.at[own_rows, :],
            send_sem=z_send.at[which, k - 1],
            recv_sem=z_recv.at[which, k - 1],
            device_id={"tensor": lax.rem(me_z + k, n_z)},
            device_id_type=MESH,
        )

    for which in range(2):
        for k in range(1, n_z):
            gather_copy(which, k).start()
    tok_all[own_rows, :] = tok_ref[...]
    cot_all[own_rows, :] = cot_ref[...]
    for which in range(2):
        for k in range(1, n_z):
            gather_copy(which, k).wait_recv()

    def core_copy(c):
        return pltpu.make_async_remote_copy(
            src_ref=csend.at[c], dst_ref=crecv.at[c],
            send_sem=c_send.at[c], recv_sem=c_recv.at[c],
            device_id={"dp": other_core}, device_id_type=MESH,
        )

    def chip_copy(c):
        return pltpu.make_async_remote_copy(
            src_ref=xsend.at[c], dst_ref=xrecv.at[c],
            send_sem=x_send.at[c], recv_sem=x_recv.at[c],
            device_id={"dp": other_chip}, device_id_type=MESH,
        )

    kept = pl.ds(pl.multiple_of(core * half, half), half)
    given = pl.ds(pl.multiple_of((1 - core) * half, half), half)

    def hidden_copy(c):
        return pltpu.make_async_remote_copy(
            src_ref=h_all.at[c, :, kept, :], dst_ref=h_all.at[c, :, kept, :],
            send_sem=h_send.at[c], recv_sem=h_recv.at[c],
            device_id={"dp": other_core}, device_id_type=MESH,
        )

    def forward(c):
        for copy in weight_copies(c):
            copy.wait()
        for j in range(3):
            src = cot_all if j == 2 else tok_all
            for dst, sel in ((csend, given), (mine, kept)):
                lhs = src[sel, :]
                if j == 2:
                    out = lax.dot_general(lhs, wd[c], NT, preferred_element_type=jnp.float32)
                else:
                    out = jnp.dot(lhs, (wg, wu)[j][c], preferred_element_type=jnp.float32)
                dst[c, j] = out.astype(dst.dtype)
        core_copy(c).start()

    def pair_sum(c):
        core_copy(c).wait_recv()
        xsend[c] = (mine[c] + crecv[c].astype(jnp.float32)).astype(xsend.dtype)
        chip_copy(c).start()

    @pl.loop(0, n_chunks)
    def _(c):
        forward(c)

        @pl.when(c >= 1)
        def _():
            pair_sum(c - 1)

    pair_sum(n_chunks - 1)

    alive = jnp.float32(0.0)
    for i in range(members_ref.shape[0]):
        alive = alive + jnp.where(members_ref[i] == me_z, 1.0, 0.0).astype(jnp.float32)

    def activate_chunk(c):
        chip_copy(c).wait_recv()
        step = 16
        for r in range(0, half, step):
            sums = [
                xsend[c, j, r : r + step].astype(jnp.float32)
                + xrecv[c, j, r : r + step].astype(jnp.float32)
                for j in range(3)
            ]
            active, slope = gelu_pair(sums[0])
            at = pl.ds(pl.multiple_of(core * half + r, step), step)
            h_all[c, 0, at, :] = (alive * active * sums[1]).astype(h_all.dtype)
            h_all[c, 1, at, :] = (alive * sums[2] * sums[1] * slope).astype(h_all.dtype)
            h_all[c, 2, at, :] = (alive * sums[2] * active).astype(h_all.dtype)
        hidden_copy(c).start()

    def token_grad(c):
        hidden_copy(c).wait_recv()
        acc[...] += lax.dot_general(
            h_all[c, 1], wg[c], NT, preferred_element_type=jnp.float32
        ) + lax.dot_general(h_all[c, 2], wu[c], NT, preferred_element_type=jnp.float32)

    acc[...] = jnp.zeros_like(acc)

    @pl.loop(0, n_chunks)
    def _(c):
        activate_chunk(c)

        @pl.when(c >= 1)
        def _():
            token_grad(c - 1)

    token_grad(n_chunks - 1)
    for k in range(n_z):
        to = lax.rem(me_z + k, n_z)
        blocks[k][...] = acc[pl.ds(pl.multiple_of(to * rows, rows), rows), :].astype(
            blocks[k].dtype
        )

    for which in range(2):
        for k in range(1, n_z):
            gather_copy(which, k).wait_send()

    @pl.loop(0, n_chunks)
    def _(c):
        core_copy(c).wait_send()
        chip_copy(c).wait_send()
        hidden_copy(c).wait_send()


def exchange(tok, cot, members, wg, wu, wd, n_z, n_chunks):
    rows, depth = tok.shape
    units = wg.shape[1]
    width = units // n_chunks
    all_rows = rows * n_z
    half = all_rows // 2
    bf16, f32 = jnp.bfloat16, jnp.float32
    vmem = pl.BlockSpec(memory_space=pltpu.VMEM)
    hbm = pl.BlockSpec(memory_space=pl.ANY)
    dma = pltpu.SemaphoreType.DMA
    part = (n_chunks, 3, half, width)
    return pl.pallas_call(
        functools.partial(exchange_kernel, n_z, n_chunks),
        out_shape=[
            jax.ShapeDtypeStruct((all_rows, depth), bf16),
            jax.ShapeDtypeStruct((all_rows, depth), bf16),
            jax.ShapeDtypeStruct((n_chunks, 3, all_rows, width), bf16),
            jax.ShapeDtypeStruct((rows, depth), f32),
        ]
        + [jax.ShapeDtypeStruct((rows, depth), bf16)] * (n_z - 1),
        in_specs=[vmem, vmem, pl.BlockSpec(memory_space=pltpu.SMEM), hbm, hbm, hbm],
        out_specs=[vmem] * (3 + n_z),
        scratch_shapes=[
            pltpu.VMEM((n_chunks, depth, width), bf16),
            pltpu.VMEM((n_chunks, depth, width), bf16),
            pltpu.VMEM((n_chunks, width, depth), bf16),
            pltpu.VMEM(part, f32),
            pltpu.VMEM(part, bf16),
            pltpu.VMEM(part, bf16),
            pltpu.VMEM(part, bf16),
            pltpu.VMEM(part, bf16),
            pltpu.VMEM((all_rows, depth), f32),
            dma((3, n_chunks)),
            dma((2, n_z - 1)),
            dma((2, n_z - 1)),
            dma((n_chunks,)),
            dma((n_chunks,)),
            dma((n_chunks,)),
            dma((n_chunks,)),
            dma((n_chunks,)),
            dma((n_chunks,)),
        ],
        compiler_params=pltpu.CompilerParams(
            collective_id=0, has_side_effects=True, vmem_limit_bytes=60 * 2**20
        ),
        cost_estimate=pl.CostEstimate(
            flops=10 * all_rows * depth * units,
            bytes_accessed=6 * depth * units,
            transcendentals=half * units,
        ),
    )(tok, cot, members, wg, wu, wd)


def weight_grads_kernel(tok_ref, cot_ref, h_ref, gate_ref, up_ref, down_ref, tok_t):
    @pl.when(pl.program_id(0) == 0)
    def _():
        tok_t[...] = tok_ref[...].T

    gate_ref[...] = jnp.dot(
        tok_t[...], h_ref[0, 1], preferred_element_type=jnp.float32
    ).astype(gate_ref.dtype)
    up_ref[...] = jnp.dot(tok_t[...], h_ref[0, 2], preferred_element_type=jnp.float32).astype(
        up_ref.dtype
    )
    down_ref[...] = lax.dot_general(
        h_ref[0, 0], cot_ref[...], TN, preferred_element_type=jnp.float32
    ).astype(down_ref.dtype)


def weight_grads(tok_all, cot_all, h_all):
    all_rows, depth = tok_all.shape
    n_chunks, _, _, width = h_all.shape
    units = n_chunks * width
    bf16 = jnp.bfloat16
    whole = pl.BlockSpec((all_rows, depth), lambda c: (0, 0))
    return pl.pallas_call(
        weight_grads_kernel,
        grid=(n_chunks,),
        out_shape=[
            jax.ShapeDtypeStruct((depth, units), bf16),
            jax.ShapeDtypeStruct((depth, units), bf16),
            jax.ShapeDtypeStruct((units, depth), bf16),
        ],
        in_specs=[whole, whole, pl.BlockSpec((1, 3, all_rows, width), lambda c: (c, 0, 0, 0))],
        out_specs=[
            pl.BlockSpec((depth, width), lambda c: (0, c)),
            pl.BlockSpec((depth, width), lambda c: (0, c)),
            pl.BlockSpec((width, depth), lambda c: (c, 0)),
        ],
        scratch_shapes=[pltpu.VMEM((depth, all_rows), bf16)],
        compiler_params=pltpu.CompilerParams(vmem_limit_bytes=40 * 2**20),
        cost_estimate=pl.CostEstimate(
            flops=6 * all_rows * depth * units,
            bytes_accessed=6 * depth * units,
            transcendentals=0,
        ),
    )(tok_all, cot_all, h_all)


def fused_body(n_z, n_chunks, tok, cot, members, wg, wu, wd):
    tok_all, cot_all, h_all, *blocks = exchange(tok, cot, members, wg, wu, wd, n_z, n_chunks)
    arrived = [
        lax.ppermute(blocks[k], "tensor", [(i, (i + k) % n_z) for i in range(n_z)])
        for k in range(1, n_z)
    ]
    grad_gate, grad_up, grad_down = weight_grads(tok_all, cot_all, h_all)
    total = blocks[0]
    for block in arrived:
        total = total + block.astype(jnp.float32)
    return total.astype(jnp.bfloat16), grad_gate, grad_up, grad_down


def solution(mesh):
    n_z, n_dp = mesh.shape["tensor"], mesh.shape["dp"]
    body = functools.partial(fused_body, n_z, 9) if n_dp == 4 and n_z == 4 else plain_body
    return jax.shard_map(
        body,
        mesh=mesh,
        in_specs=(
            P(("groups", "tensor"), "dp"),
            P(("groups", "tensor"), "dp"),
            P(),
            P("dp", "tensor"),
            P("dp", "tensor"),
            P("tensor", "dp"),
        ),
        out_specs=(
            P(("groups", "tensor"), "dp"),
            P(("groups", "dp"), "tensor"),
            P(("groups", "dp"), "tensor"),
            P(("groups", "tensor"), "dp"),
        ),
        check_vma=False,
    )
```

```python
import functools
import math

import jax
import jax.numpy as jnp
from jax import lax
from jax.experimental import pallas as pl
from jax.experimental.pallas import tpu as pltpu
from jax.sharding import PartitionSpec as P

cubic_coef = 0.044715


def gelu_pair(pre_act):
    tanh_scale = math.sqrt(2.0 / math.pi)
    tangent = jnp.tanh(tanh_scale * (pre_act + cubic_coef * pre_act * pre_act * pre_act))
    active = 0.5 * pre_act * (1.0 + tangent)
    slope_val = 0.5 * (1.0 + tangent) + 0.5 * pre_act * (1.0 - tangent * tangent) * tanh_scale * (
        1.0 + 3.0 * cubic_coef * pre_act * pre_act
    )
    return (active, slope_val)


def activate(totals, retained_marker):
    gate_sum = totals[:, 0]
    up_sum = totals[:, 1]
    back_sum = totals[:, 2]
    active, slope_val = gelu_pair(gate_sum)
    hidden = (retained_marker * active * up_sum).astype(jnp.bfloat16)
    gate_grad = (retained_marker * back_sum * up_sum * slope_val).astype(jnp.bfloat16)
    up_grad = (retained_marker * back_sum * active).astype(jnp.bfloat16)
    return (hidden, gate_grad, up_grad)


def plain_body(
    incoming_entries,
    output_adjoint,
    remaining_members,
    gating_matrix,
    expansion_matrix,
    contraction_matrix,
):
    cycle_location = lax.axis_index("tensor")
    retained_marker = jnp.sum((remaining_members == cycle_location).astype(jnp.float32))
    tok_all, cot_all = (
        lax.all_gather(incoming_entries, "tensor", axis=0, tiled=True),
        lax.all_gather(output_adjoint, "tensor", axis=0, tiled=True),
    )
    gate_part = jnp.dot(tok_all, gating_matrix, preferred_element_type=jnp.float32)
    up_part = jnp.dot(tok_all, expansion_matrix, preferred_element_type=jnp.float32)
    back_part = lax.dot_general(
        cot_all, contraction_matrix, (((1,), (1,)), ((), ())), preferred_element_type=jnp.float32
    )
    totals = lax.psum_scatter(
        jnp.stack([gate_part, up_part, back_part], axis=1).astype(jnp.bfloat16),
        "dp",
        scatter_dimension=0,
        tiled=True,
    ).astype(jnp.float32)
    hidden_loc, gate_loc, up_loc = activate(totals, retained_marker)
    hidden, gate_grad, up_grad = (
        lax.all_gather(hidden_loc, "dp", axis=0, tiled=True),
        lax.all_gather(gate_loc, "dp", axis=0, tiled=True),
        lax.all_gather(up_loc, "dp", axis=0, tiled=True),
    )
    over_rows = (((0,), (0,)), ((), ()))
    grad_gate = lax.dot_general(
        tok_all, gate_grad, over_rows, preferred_element_type=jnp.float32
    ).astype(jnp.bfloat16)
    grad_up = lax.dot_general(
        tok_all, up_grad, over_rows, preferred_element_type=jnp.float32
    ).astype(jnp.bfloat16)
    grad_down = lax.dot_general(
        hidden, cot_all, over_rows, preferred_element_type=jnp.float32
    ).astype(jnp.bfloat16)
    over_units = (((1,), (1,)), ((), ()))
    first = lax.dot_general(
        gate_grad, gating_matrix, over_units, preferred_element_type=jnp.float32
    )
    second = lax.dot_general(
        up_grad, expansion_matrix, over_units, preferred_element_type=jnp.float32
    )
    grad_tokens = lax.psum_scatter(
        (first + second).astype(jnp.bfloat16), "tensor", scatter_dimension=0, tiled=True
    )
    return (grad_tokens, grad_gate, grad_up, grad_down)


MESH = pl.DeviceIdType.MESH
NT = (((1,), (1,)), ((), ()))
TN = (((0,), (0,)), ((), ()))


def exchange_kernel(
    n_z,
    n_chunks,
    tok_ref,
    cot_ref,
    members_ref,
    wg_hbm,
    wu_hbm,
    wd_hbm,
    tok_all,
    cot_all,
    h_all,
    *rest,
):
    blocks = rest[:n_z]
    (
        wg, wu, wd, mine, csend, crecv, xsend, xrecv, acc,
        w_sem, z_send, z_recv, c_send, c_recv, x_send, x_recv, h_send, h_recv,
    ) = rest[n_z:]
    rows = tok_ref.shape[0]
    half = mine.shape[2]
    width = wg.shape[2]
    me_z = lax.axis_index("tensor")
    me_d = lax.axis_index("dp")
    core = lax.rem(me_d, 2)
    other_core = me_d + 1 - 2 * core
    other_chip = lax.rem(me_d + 2, 4)

    def weight_copies(c):
        cols = pl.ds(pl.multiple_of(c * width, width), width)
        return (
            pltpu.make_async_copy(wg_hbm.at[:, cols], wg.at[c], w_sem.at[0, c]),
            pltpu.make_async_copy(wu_hbm.at[:, cols], wu.at[c], w_sem.at[1, c]),
            pltpu.make_async_copy(wd_hbm.at[cols, :], wd.at[c], w_sem.at[2, c]),
        )

    @pl.loop(0, n_chunks)
    def _(c):
        for copy in weight_copies(c):
            copy.start()

    barrier = pltpu.get_barrier_semaphore()
    for k in range(1, n_z):
        pl.semaphore_signal(
            barrier, inc=1, device_id={"tensor": lax.rem(me_z + k, n_z)}, device_id_type=MESH
        )
    pl.semaphore_signal(barrier, inc=1, device_id={"dp": other_core}, device_id_type=MESH)
    pl.semaphore_signal(barrier, inc=1, device_id={"dp": other_chip}, device_id_type=MESH)
    pl.semaphore_wait(barrier, n_z + 1)

    def place(rank):
        per_half = n_z // 2
        slot = lax.rem(rank // per_half + core, 2) * per_half + lax.rem(rank, per_half)
        return pl.ds(pl.multiple_of(slot * rows, rows), rows)

    own_rows = place(me_z)

    def gather_copy(which, k):
        src, dst = ((tok_ref, tok_all), (cot_ref, cot_all))[which]
        return pltpu.make_async_remote_copy(
            src_ref=src,
            dst_ref=dst.at[own_rows, :],
            send_sem=z_send.at[which, k - 1],
            recv_sem=z_recv.at[which, k - 1],
            device_id={"tensor": lax.rem(me_z + k, n_z)},
            device_id_type=MESH,
        )

    for which in range(2):
        for k in range(1, n_z):
            gather_copy(which, k).start()
    tok_all[own_rows, :] = tok_ref[...]
    cot_all[own_rows, :] = cot_ref[...]
    for which in range(2):
        for k in range(1, n_z):
            gather_copy(which, k).wait_recv()

    def core_copy(c):
        return pltpu.make_async_remote_copy(
            src_ref=csend.at[c], dst_ref=crecv.at[c],
            send_sem=c_send.at[c], recv_sem=c_recv.at[c],
            device_id={"dp": other_core}, device_id_type=MESH,
        )

    def chip_copy(c):
        return pltpu.make_async_remote_copy(
            src_ref=xsend.at[c], dst_ref=xrecv.at[c],
            send_sem=x_send.at[c], recv_sem=x_recv.at[c],
            device_id={"dp": other_chip}, device_id_type=MESH,
        )

    def hidden_copy(c):
        return pltpu.make_async_remote_copy(
            src_ref=h_all.at[c, :, :half, :], dst_ref=h_all.at[c, :, half:, :],
            send_sem=h_send.at[c], recv_sem=h_recv.at[c],
            device_id={"dp": other_core}, device_id_type=MESH,
        )

    def forward(c):
        for copy in weight_copies(c):
            copy.wait()
        for j in range(3):
            if j == 2:
                out = lax.dot_general(
                    cot_all[...], wd[c], NT, preferred_element_type=jnp.float32
                )
            else:
                out = jnp.dot(tok_all[...], (wg, wu)[j][c], preferred_element_type=jnp.float32)
            mine[c, j] = out[:half]
            csend[c, j] = out[half:].astype(csend.dtype)
        core_copy(c).start()

    def pair_sum(c):
        core_copy(c).wait_recv()
        xsend[c] = (mine[c] + crecv[c].astype(jnp.float32)).astype(xsend.dtype)
        chip_copy(c).start()

    @pl.loop(0, n_chunks)
    def _(c):
        forward(c)

        @pl.when(c >= 1)
        def _():
            pair_sum(c - 1)

    pair_sum(n_chunks - 1)

    alive = jnp.float32(0.0)
    for i in range(members_ref.shape[0]):
        alive = alive + jnp.where(members_ref[i] == me_z, 1.0, 0.0).astype(jnp.float32)

    def activate_chunk(c):
        chip_copy(c).wait_recv()
        step = 16
        for r in range(0, half, step):
            sums = [
                xsend[c, j, r : r + step].astype(jnp.float32)
                + xrecv[c, j, r : r + step].astype(jnp.float32)
                for j in range(3)
            ]
            active, slope = gelu_pair(sums[0])
            at = slice(r, r + step)
            h_all[c, 0, at, :] = (alive * active * sums[1]).astype(h_all.dtype)
            h_all[c, 1, at, :] = (alive * sums[2] * sums[1] * slope).astype(h_all.dtype)
            h_all[c, 2, at, :] = (alive * sums[2] * active).astype(h_all.dtype)
        hidden_copy(c).start()

    def token_grad(c):
        hidden_copy(c).wait_recv()
        acc[...] += lax.dot_general(
            h_all[c, 1], wg[c], NT, preferred_element_type=jnp.float32
        ) + lax.dot_general(h_all[c, 2], wu[c], NT, preferred_element_type=jnp.float32)

    acc[...] = jnp.zeros_like(acc)

    @pl.loop(0, n_chunks)
    def _(c):
        activate_chunk(c)

        @pl.when(c >= 1)
        def _():
            token_grad(c - 1)

    token_grad(n_chunks - 1)
    for k in range(n_z):
        to = lax.rem(me_z + k, n_z)
        blocks[k][...] = acc[place(to), :].astype(
            blocks[k].dtype
        )

    for which in range(2):
        for k in range(1, n_z):
            gather_copy(which, k).wait_send()

    @pl.loop(0, n_chunks)
    def _(c):
        core_copy(c).wait_send()
        chip_copy(c).wait_send()
        hidden_copy(c).wait_send()


def exchange(tok, cot, members, wg, wu, wd, n_z, n_chunks):
    rows, depth = tok.shape
    units = wg.shape[1]
    width = units // n_chunks
    all_rows = rows * n_z
    half = all_rows // 2
    bf16, f32 = jnp.bfloat16, jnp.float32
    vmem = pl.BlockSpec(memory_space=pltpu.VMEM)
    hbm = pl.BlockSpec(memory_space=pl.ANY)
    dma = pltpu.SemaphoreType.DMA
    part = (n_chunks, 3, half, width)
    return pl.pallas_call(
        functools.partial(exchange_kernel, n_z, n_chunks),
        out_shape=[
            jax.ShapeDtypeStruct((all_rows, depth), bf16),
            jax.ShapeDtypeStruct((all_rows, depth), bf16),
            jax.ShapeDtypeStruct((n_chunks, 3, all_rows, width), bf16),
            jax.ShapeDtypeStruct((rows, depth), f32),
        ]
        + [jax.ShapeDtypeStruct((rows, depth), bf16)] * (n_z - 1),
        in_specs=[vmem, vmem, pl.BlockSpec(memory_space=pltpu.SMEM), hbm, hbm, hbm],
        out_specs=[vmem] * (3 + n_z),
        scratch_shapes=[
            pltpu.VMEM((n_chunks, depth, width), bf16),
            pltpu.VMEM((n_chunks, depth, width), bf16),
            pltpu.VMEM((n_chunks, width, depth), bf16),
            pltpu.VMEM(part, f32),
            pltpu.VMEM(part, bf16),
            pltpu.VMEM(part, bf16),
            pltpu.VMEM(part, bf16),
            pltpu.VMEM(part, bf16),
            pltpu.VMEM((all_rows, depth), f32),
            dma((3, n_chunks)),
            dma((2, n_z - 1)),
            dma((2, n_z - 1)),
            dma((n_chunks,)),
            dma((n_chunks,)),
            dma((n_chunks,)),
            dma((n_chunks,)),
            dma((n_chunks,)),
            dma((n_chunks,)),
        ],
        compiler_params=pltpu.CompilerParams(
            collective_id=0, has_side_effects=True, vmem_limit_bytes=60 * 2**20
        ),
        cost_estimate=pl.CostEstimate(
            flops=10 * all_rows * depth * units,
            bytes_accessed=6 * depth * units,
            transcendentals=half * units,
        ),
    )(tok, cot, members, wg, wu, wd)


def weight_grads_kernel(tok_ref, cot_ref, h_ref, gate_ref, up_ref, down_ref, tok_t):
    @pl.when(pl.program_id(0) == 0)
    def _():
        tok_t[...] = tok_ref[...].T

    gate_ref[...] = jnp.dot(
        tok_t[...], h_ref[0, 1], preferred_element_type=jnp.float32
    ).astype(gate_ref.dtype)
    up_ref[...] = jnp.dot(tok_t[...], h_ref[0, 2], preferred_element_type=jnp.float32).astype(
        up_ref.dtype
    )
    down_ref[...] = lax.dot_general(
        h_ref[0, 0], cot_ref[...], TN, preferred_element_type=jnp.float32
    ).astype(down_ref.dtype)


def weight_grads(tok_all, cot_all, h_all):
    all_rows, depth = tok_all.shape
    n_chunks, _, _, width = h_all.shape
    units = n_chunks * width
    bf16 = jnp.bfloat16
    whole = pl.BlockSpec((all_rows, depth), lambda c: (0, 0))
    return pl.pallas_call(
        weight_grads_kernel,
        grid=(n_chunks,),
        out_shape=[
            jax.ShapeDtypeStruct((depth, units), bf16),
            jax.ShapeDtypeStruct((depth, units), bf16),
            jax.ShapeDtypeStruct((units, depth), bf16),
        ],
        in_specs=[whole, whole, pl.BlockSpec((1, 3, all_rows, width), lambda c: (c, 0, 0, 0))],
        out_specs=[
            pl.BlockSpec((depth, width), lambda c: (0, c)),
            pl.BlockSpec((depth, width), lambda c: (0, c)),
            pl.BlockSpec((width, depth), lambda c: (c, 0)),
        ],
        scratch_shapes=[pltpu.VMEM((depth, all_rows), bf16)],
        compiler_params=pltpu.CompilerParams(vmem_limit_bytes=60 * 2**20),
        cost_estimate=pl.CostEstimate(
            flops=6 * all_rows * depth * units,
            bytes_accessed=6 * depth * units,
            transcendentals=0,
        ),
    )(tok_all, cot_all, h_all)


def fused_body(n_z, n_chunks, tok, cot, members, wg, wu, wd):
    tok_all, cot_all, h_all, *blocks = exchange(tok, cot, members, wg, wu, wd, n_z, n_chunks)
    arrived = [
        lax.ppermute(blocks[k], "tensor", [(i, (i + k) % n_z) for i in range(n_z)])
        for k in range(1, n_z)
    ]
    grad_gate, grad_up, grad_down = weight_grads(tok_all, cot_all, h_all)
    total = blocks[0]
    for block in arrived:
        total = total + block.astype(jnp.float32)
    return total.astype(jnp.bfloat16), grad_gate, grad_up, grad_down


def solution(mesh):
    n_z, n_dp = mesh.shape["tensor"], mesh.shape["dp"]
    body = functools.partial(fused_body, n_z, 9) if n_dp == 4 and n_z == 4 else plain_body
    return jax.shard_map(
        body,
        mesh=mesh,
        in_specs=(
            P(("groups", "tensor"), "dp"),
            P(("groups", "tensor"), "dp"),
            P(),
            P("dp", "tensor"),
            P("dp", "tensor"),
            P("tensor", "dp"),
        ),
        out_specs=(
            P(("groups", "tensor"), "dp"),
            P(("groups", "dp"), "tensor"),
            P(("groups", "dp"), "tensor"),
            P(("groups", "tensor"), "dp"),
        ),
        check_vma=False,
    )
```
